512 devices in a mesh: ctx: 64 (over z, y_lo, core), ch: 8 (over y_hi, x).
Axes of the slice: x: 4, y: 8 (y_hi: 2, y_lo: 4; y = y_hi * 4 + y_lo), z: 8, core: 2. Of those that a mesh axis runs over, the one named last changes fastest.
Arguments:
- hidden: bfloat16 [8192, 8192], P('ctx', 'ch'), may hold values from -2000 to 2000
- gating: bfloat16 [8192, 8192], P('ctx', 'ch'), may hold values from -6 to 6
- filter_taps: bfloat16 [8192, 8192], P('ctx', 'ch'), may hold values from -181.01934 to 181.01934
- norm_gain: float32 [8192], P('ch'), may hold values from 0.25 to 1.75
- upstream: bfloat16 [8192, 8192], P('ctx', 'ch'), may hold values from -6 to 6
Outputs:
- output: bfloat16 [8192, 8192], P('ctx', 'ch')
- gate_grad: bfloat16 [8192, 8192], P('ctx', 'ch')
- filter_grad: bfloat16 [8192, 8192], P('ctx', 'ch')
- hidden_grad: bfloat16 [8192, 8192], P('ctx', 'ch')
The draws below stay inside these ranges and needn't reach their ends.
All inputs are finite; a program needn't handle non-finite values.
Results may differ from the reference program's by a relative error of at most 0.0058.
Values may be sent and summed in bfloat16 or wider, within the bound.
A program may use at most 64 MiB of HBM per device.

```python
import math
import jax
import jax.numpy as jnp
from jax import lax

FEATURE_WIDTH = 8192
TOKEN_TOTAL = 8192


def draw_hidden(key, part):
    key = jax.random.fold_in(key, 11)
    stochastic_seeds = jax.random.split(key, 3)
    channel_ramp = jnp.arange(FEATURE_WIDTH, dtype=jnp.float32) / FEATURE_WIDTH
    row_scale = 10.0 ** jax.random.uniform(stochastic_seeds[1], (TOKEN_TOTAL, 1), dtype=jnp.float32)
    column_scale = 10.0 ** jax.random.uniform(stochastic_seeds[2], (1, FEATURE_WIDTH), dtype=jnp.float32)
    noise_values = jnp.clip(jax.random.normal(stochastic_seeds[0], (TOKEN_TOTAL, FEATURE_WIDTH), dtype=jnp.float32), -6.0, 6.0)
    growth = 3.0 ** channel_ramp
    return (noise_values * row_scale * column_scale * growth[None, :]).astype(jnp.bfloat16)


def draw_filter_taps(key, part):
    key = jax.random.fold_in(key, 23)
    stochastic_seeds = jax.random.split(key, 6)
    token_ordinal = jnp.arange(TOKEN_TOTAL, dtype=jnp.float32)[:, None]
    slow_rate = jnp.exp(jax.random.uniform(stochastic_seeds[0], (FEATURE_WIDTH,), dtype=jnp.float32, minval=math.log(0.2 / TOKEN_TOTAL), maxval=math.log(2.0 / TOKEN_TOTAL)))
    fast_rate = jnp.exp(jax.random.uniform(stochastic_seeds[1], (FEATURE_WIDTH,), dtype=jnp.float32, minval=math.log(4.0 / TOKEN_TOTAL), maxval=math.log(1.0 / 30.0)))
    chooser = jax.random.uniform(stochastic_seeds[2], (FEATURE_WIDTH,), dtype=jnp.float32)
    slow_share = 0.5
    noise_values = jnp.clip(jax.random.normal(stochastic_seeds[5], (TOKEN_TOTAL, FEATURE_WIDTH), dtype=jnp.float32), -6.0, 6.0)
    rates = jnp.where(chooser < slow_share, slow_rate, fast_rate)
    spike_start_step = jax.random.randint(stochastic_seeds[3], (3,), 0, TOKEN_TOTAL).astype(jnp.float32)
    spike_window_flag = jax.random.uniform(stochastic_seeds[4], (3, FEATURE_WIDTH), dtype=jnp.float32, minval=0.5, maxval=0.8)
    fading_profile = jnp.exp(-rates[None, :] * token_ordinal)
    for kernel_spike in range(3):
        fading_profile = fading_profile * jnp.where(token_ordinal >= spike_start_step[kernel_spike], spike_window_flag[kernel_spike][None, :], 1.0)
    energy = jnp.expm1(-2.0 * rates * TOKEN_TOTAL) / jnp.expm1(-2.0 * rates)
    scaling = jnp.sqrt(TOKEN_TOTAL / energy)
    return (noise_values * fading_profile * scaling[None, :]).astype(jnp.bfloat16)


def level_of(key, shape, shards, low, largest):
    loudness, own = 1.0, jax.random.fold_in(key, 6)
    for axis_at, shards_of in shards:
        steps = jnp.exp(jax.random.uniform(jax.random.fold_in(own, axis_at), (shards_of,), jnp.float32, low / len(shards), largest / len(shards)))
        loudness = loudness * jnp.repeat(steps, shape[axis_at] // shards_of).reshape([-1 if axis == axis_at else 1 for axis in range(len(shape))])
    return loudness


def noise(stream_key, extent, spread, reach, cuts=(), kind=jnp.bfloat16):
    drawn = spread * jax.random.normal(stream_key, extent, jnp.float32)
    if cuts:
        drawn = drawn * level_of(stream_key, extent, cuts, -0.22, 0.18)
    return jnp.clip(drawn, -reach, reach).astype(kind)


def setup_inputs(seed: int = 0) -> dict:
    arg_keys = jax.random.split(jax.random.key(seed), 6)
    hidden = draw_hidden(jax.random.fold_in(arg_keys[5], 71), 0)
    gating = noise(arg_keys[1], (TOKEN_TOTAL, FEATURE_WIDTH), 1.0, 6.0, ((0, 64), (1, 8)))
    filter_taps = draw_filter_taps(jax.random.fold_in(arg_keys[5], 71), 0)
    norm_gain = jnp.clip(1.0 + 0.15 * jax.random.normal(arg_keys[3], (FEATURE_WIDTH,), jnp.float32), 0.25, 1.75)
    upstream = noise(arg_keys[4], (TOKEN_TOTAL, FEATURE_WIDTH), 1.0, 6.0, ((0, 64), (1, 8)))
    return dict(hidden=hidden, gating=gating, filter_taps=filter_taps, norm_gain=norm_gain, upstream=upstream)


epsilon = 1e-06

def reference(hidden, gating, filter_taps, norm_gain, upstream):
    length = hidden.shape[0]
    widened = hidden.astype(jnp.float32)
    inverse_rms = lax.rsqrt(lax.optimization_barrier(jnp.mean(widened * widened, axis=1)) + epsilon)
    normed = widened * inverse_rms[:, None]
    mixed_in = (normed * norm_gain[None, :]).astype(jnp.bfloat16)
    gate_wide = gating.astype(jnp.float32)
    upstream_wide = upstream.astype(jnp.float32)
    conv_grad = (upstream_wide * gate_wide).astype(jnp.bfloat16)
    block_width = min(FEATURE_WIDTH, 512)
    factor = 1.0 / math.sqrt(length)

    def per_block(block_index):
        offset = (block_index * block_width).astype(jnp.int32)

        def column_block(array):
            return lax.dynamic_slice_in_dim(array, offset, block_width, 1).astype(jnp.float32)
        mixed_spec = jnp.fft.rfft(column_block(mixed_in), n=2 * length, axis=0)
        filter_spec = jnp.fft.rfft(column_block(filter_taps), n=2 * length, axis=0)
        grad_spec = jnp.fft.rfft(column_block(conv_grad), n=2 * length, axis=0)

        def restore(spectrum):
            return jnp.fft.irfft(spectrum, n=2 * length, axis=0)[:length] * factor
        return (restore(mixed_spec * filter_spec), restore(jnp.conj(filter_spec) * grad_spec), restore(jnp.conj(mixed_spec) * grad_spec))
    blocks = lax.map(per_block, jnp.arange(FEATURE_WIDTH // block_width, dtype=jnp.int32))

    def unblock(stacked):
        return jnp.moveaxis(stacked, 0, 1).reshape(length, FEATURE_WIDTH)
    convolved = unblock(blocks[0])
    mixed_grad = unblock(blocks[1])
    taps_grad = unblock(blocks[2])
    output = (gate_wide * convolved).astype(jnp.bfloat16)
    gate_grad = (upstream_wide * convolved).astype(jnp.bfloat16)
    scaled_grad = mixed_grad * norm_gain[None, :]
    projection = lax.optimization_barrier(jnp.mean(scaled_grad * normed, axis=1))
    hidden_grad = (inverse_rms[:, None] * (scaled_grad - normed * projection[:, None])).astype(jnp.bfloat16)
    return (output, gate_grad, taps_grad.astype(jnp.bfloat16), hidden_grad)
```

```python
import functools
import math

import jax
import jax.numpy as jnp
import numpy as np
from jax import lax
from jax.experimental import pallas as pl
from jax.experimental.pallas import tpu as pltpu
from jax.sharding import PartitionSpec as P

MESH = pl.DeviceIdType.MESH
EPSILON = 1e-06
F32, BF16 = jnp.float32, jnp.bfloat16

WIDTH = 8192
CTX, CH = 64, 8
ROWS = 128
COLS = 1024
OWN = 16
LENGTH = CTX * ROWS


def split(values):
    high = values.astype(BF16)
    return high, (values - high.astype(F32)).astype(BF16)


def split_table(values):
    high = np.asarray(values, np.float32).astype(jnp.bfloat16)
    low = (np.asarray(values, np.float64) - high.astype(np.float64)).astype(jnp.bfloat16)
    return high, low


def tables():
    wave = np.arange(CTX)[:, None] + 0.25
    block = 2.0 * np.pi * wave * np.arange(CTX)[None, :] / CTX
    twist = 2.0 * np.pi * wave * np.arange(ROWS)[None, :] / LENGTH
    inner = 2.0 * np.pi * np.arange(ROWS)[:, None] * np.arange(ROWS)[None, :] / ROWS
    outer = np.concatenate([np.cos(block), -np.sin(block)], 0)
    dense = np.block([[np.cos(inner), -np.sin(inner)], [np.sin(inner), np.cos(inner)]])
    factor = 1.0 / (math.sqrt(LENGTH) * LENGTH)
    back = outer.T * factor
    outer_hi, outer_lo = split_table(outer)
    back_hi, back_lo = split_table(back)
    dense_hi, dense_lo = split_table(dense)
    turned_hi, turned_lo = split_table(dense.T)
    return (
        np.concatenate([outer_hi, outer_lo], 1),
        np.concatenate([back_hi, back_hi, back_lo], 1),
        np.stack([dense_hi, dense_lo]),
        np.stack([turned_hi, turned_lo]),
        np.stack([np.cos(twist), np.sin(twist)]).astype(np.float32),
    )


def dot(a, b):
    return jnp.dot(a, b, preferred_element_type=F32)


def kernel(
    hidden_hbm, gating_hbm, taps_hbm, upstream_hbm, gain_ref, outer_ref, back_ref, dense_ref, turned_ref, twist_ref,
    output_hbm, gate_grad_hbm, filter_grad_hbm, hidden_grad_hbm,
    hidden, gating, taps, upstream,
    output, gate_grad, filter_grad, hidden_grad,
    send, recv, spec, part_hi, part_lo, wide, stage, hidden_t, gain_t, sums, sums_in,
    load_sem, store_sem, send_sem, recv_sem, sum_send, sum_recv,
):
    me, mych = lax.axis_index("ctx"), lax.axis_index("ch")
    loads = [
        pltpu.make_async_copy(src, dst, load_sem.at[i])
        for i, (src, dst) in enumerate(
            ((taps_hbm, taps), (hidden_hbm, hidden), (upstream_hbm, upstream), (gating_hbm, gating))
        )
    ]
    for load in loads:
        load.start()

    barrier = pltpu.get_barrier_semaphore()

    def greet(i, carry):
        peer = lax.rem(me + i, CTX)
        pl.semaphore_signal(barrier, inc=1, device_id={"ctx": peer}, device_id_type=MESH)
        return carry

    def greet_ch(i, carry):
        peer = lax.rem(mych + i, CH)
        pl.semaphore_signal(barrier, inc=1, device_id={"ch": peer}, device_id_type=MESH)
        return carry

    lax.fori_loop(1, CTX, greet, 0)
    lax.fori_loop(1, CH, greet_ch, 0)

    def exchange(a):
        recv[a, me] = send[a, me]

        def one(i, carry):
            peer = lax.rem(me + i, CTX)
            pltpu.make_async_remote_copy(
                src_ref=send.at[a, peer], dst_ref=recv.at[a, me], send_sem=send_sem.at[a], recv_sem=recv_sem.at[a],
                device_id={"ctx": peer}, device_id_type=MESH,
            ).start()
            return carry

        lax.fori_loop(1, CTX, one, 0)

    def whole(a):
        rest = pl.ds(0, CTX - 1)
        return pltpu.make_async_remote_copy(
            src_ref=send.at[a, rest], dst_ref=recv.at[a, rest], send_sem=send_sem.at[a], recv_sem=recv_sem.at[a],
            device_id={"ctx": lax.rem(me + 1, CTX)}, device_id_type=MESH,
        )

    def add_up(which, partial):
        sums[which] = partial
        sums_in[which, mych] = partial

        def one(i, carry):
            peer = lax.rem(mych + i, CH)
            pltpu.make_async_remote_copy(
                src_ref=sums.at[which], dst_ref=sums_in.at[which, mych],
                send_sem=sum_send.at[which], recv_sem=sum_recv.at[which],
                device_id={"ch": peer}, device_id_type=MESH,
            ).start()
            return carry

        lax.fori_loop(1, CH, one, 0)

    def whole_sum(which):
        rest = pl.ds(0, CH - 1)
        return pltpu.make_async_remote_copy(
            src_ref=sums_in.at[which, rest], dst_ref=sums_in.at[which, rest],
            send_sem=sum_send.at[which], recv_sem=sum_recv.at[which],
            device_id={"ch": lax.rem(mych + 1, CH)}, device_id_type=MESH,
        )

    def added(which):
        whole_sum(which).wait_recv()
        total = jnp.sum(sums_in[which], axis=0)
        return jnp.sum(total, axis=0, keepdims=True) * (1.0 / WIDTH)

    def turn_out(a, block, values):
        send[a, pl.ds(block * 8, 8)] = jnp.transpose(values).reshape(8, OWN, ROWS).astype(BF16)

    def forward(a):
        stage[...] = recv[a].reshape(COLS, ROWS).astype(F32)

        def pair(p, carry):
            x = jnp.concatenate([stage[pl.ds(2 * p + j, CTX, stride=OWN), :].astype(BF16) for j in (0, 1)], 1)
            waves = dot(outer_ref[...], jnp.concatenate([x, x], 0))
            for j in (0, 1):
                re, im = waves[:CTX, j * ROWS : (j + 1) * ROWS], waves[CTX:, j * ROWS : (j + 1) * ROWS]
                q = jnp.concatenate(
                    [re * twist_ref[0] + im * twist_ref[1], im * twist_ref[0] - re * twist_ref[1]], 1
                )
                at = pl.ds(pl.multiple_of((2 * p + j) * CTX, CTX), CTX)
                part_hi[at, :], part_lo[at, :] = split(q)
            return carry

        lax.fori_loop(0, OWN // 2, pair, 0, unroll=2)

        def rows(b, carry):
            at = pl.ds(pl.multiple_of(b * 256, 256), 256)
            high = part_hi[at, :]
            spec[a, at, :] = dot(high, dense_ref[0]) + (dot(high, dense_ref[1]) + dot(part_lo[at, :], dense_ref[0]))
            return carry

        lax.fori_loop(0, COLS // 256, rows, 0)

    def inverse(a, first, second, conjugate):
        def rows(b, carry):
            at = pl.ds(pl.multiple_of(b * 128, 128), 128)
            fr, fi = spec[first, at, :ROWS], spec[first, at, ROWS:]
            sr, si = spec[second, at, :ROWS], spec[second, at, ROWS:]
            if conjugate:
                re, im = fr * sr + fi * si, fr * si - fi * sr
            else:
                re, im = fr * sr - fi * si, fr * si + fi * sr
            high, low = split(jnp.concatenate([re, im], 1))
            wide[at, :] = dot(high, turned_ref[0]) + (dot(high, turned_ref[1]) + dot(low, turned_ref[0]))
            return carry

        lax.fori_loop(0, COLS // 128, rows, 0)

        def pair(p, carry):
            u = []
            for j in (0, 1):
                at = pl.ds(pl.multiple_of((2 * p + j) * CTX, CTX), CTX)
                re, im = wide[at, :ROWS], wide[at, ROWS:]
                u.append(
                    jnp.concatenate(
                        [re * twist_ref[0] - im * twist_ref[1], re * twist_ref[1] + im * twist_ref[0]], 0
                    )
                )
            high, low = split(jnp.concatenate(u, 1))
            y = dot(back_ref[...], jnp.concatenate([high, low, high], 0))
            for j in (0, 1):
                stage[pl.ds(2 * p + j, CTX, stride=OWN), :] = y[:, j * ROWS : (j + 1) * ROWS]
            return carry

        lax.fori_loop(0, OWN // 2, pair, 0, unroll=2)
        send[a] = stage[...].reshape(CTX, OWN, ROWS).astype(BF16)

    blocks = [slice(i * 128, (i + 1) * 128) for i in range(COLS // 128)]

    loads[0].wait()
    for i, at in enumerate(blocks):
        turn_out(0, i, taps[:, at].astype(F32))
    pl.semaphore_wait(barrier, CTX - 1 + CH - 1)
    exchange(0)

    loads[1].wait()
    partial = jnp.zeros((8, ROWS), F32)
    for at in blocks:
        turned = jnp.transpose(hidden[:, at].astype(F32))
        hidden_t[at, :] = turned
        partial = partial + jnp.sum((turned * turned).reshape(16, 8, ROWS), axis=0)
    add_up(0, partial)

    loads[2].wait()
    loads[3].wait()
    for i, at in enumerate(blocks):
        turn_out(1, i, upstream[:, at].astype(F32) * gating[:, at].astype(F32))
    exchange(1)

    for at in blocks:
        gain_t[at, :] = jnp.transpose(jnp.broadcast_to(gain_ref[:, at], (ROWS, 128)))
    inverse_rms = lax.rsqrt(added(0) + EPSILON)
    for i, at in enumerate(blocks):
        normed = hidden_t[at, :] * inverse_rms
        hidden_t[at, :] = normed
        send[2, pl.ds(i * 8, 8)] = (normed * gain_t[at, :]).astype(BF16).reshape(8, OWN, ROWS)
    exchange(2)

    whole(0).wait_recv()
    forward(0)
    whole(1).wait_recv()
    forward(1)
    inverse(3, 0, 1, True)
    exchange(3)
    whole(2).wait_recv()
    forward(2)
    inverse(4, 2, 0, False)
    exchange(4)
    inverse(5, 2, 1, True)
    exchange(5)

    whole(3).wait_recv()
    partial = jnp.zeros((8, ROWS), F32)
    for i, at in enumerate(blocks):
        scaled = recv[3, pl.ds(i * 8, 8)].astype(F32).reshape(128, ROWS) * gain_t[at, :]
        gain_t[at, :] = scaled
        partial = partial + jnp.sum((scaled * hidden_t[at, :]).reshape(16, 8, ROWS), axis=0)
    add_up(1, partial)

    stores = [
        pltpu.make_async_copy(src, dst, store_sem.at[i])
        for i, (src, dst) in enumerate(
            (
                (output, output_hbm),
                (gate_grad, gate_grad_hbm),
                (filter_grad, filter_grad_hbm),
                (hidden_grad, hidden_grad_hbm),
            )
        )
    ]
    projection = added(1)
    for at in blocks:
        value = inverse_rms * (gain_t[at, :] - hidden_t[at, :] * projection)
        hidden_grad[:, at] = jnp.transpose(value).astype(BF16)
    stores[3].start()

    whole(4).wait_recv()
    for i, at in enumerate(blocks):
        value = jnp.transpose(recv[4, pl.ds(i * 8, 8)].astype(F32).reshape(128, ROWS))
        output[:, at] = (gating[:, at].astype(F32) * value).astype(BF16)
        gate_grad[:, at] = (upstream[:, at].astype(F32) * value).astype(BF16)
    stores[0].start()
    stores[1].start()

    whole(5).wait_recv()
    for i, at in enumerate(blocks):
        filter_grad[:, at] = jnp.transpose(recv[5, pl.ds(i * 8, 8)].astype(F32).reshape(128, ROWS)).astype(BF16)
    stores[2].start()

    for a in range(6):
        whole(a).wait_send()
    for which in (0, 1):
        whole_sum(which).wait_send()
    for store in stores:
        store.wait()


def shards(hidden, gating, filter_taps, norm_gain, upstream):
    consts = [jnp.asarray(t) for t in tables()]
    whole_array = jax.ShapeDtypeStruct((ROWS, COLS), BF16)
    vmem, hbm = pl.BlockSpec(memory_space=pltpu.VMEM), pl.BlockSpec(memory_space=pl.ANY)
    block = pltpu.VMEM((ROWS, COLS), BF16)
    return pl.pallas_call(
        kernel,
        out_shape=(whole_array,) * 4,
        in_specs=[hbm] * 4 + [vmem] * 6,
        out_specs=(hbm,) * 4,
        scratch_shapes=[block] * 8
        + [
            pltpu.VMEM((6, CTX, OWN, ROWS), BF16),
            pltpu.VMEM((6, CTX, OWN, ROWS), BF16),
            pltpu.VMEM((3, COLS, 2 * ROWS), F32),
            pltpu.VMEM((COLS, 2 * ROWS), BF16),
            pltpu.VMEM((COLS, 2 * ROWS), BF16),
            pltpu.VMEM((COLS, 2 * ROWS), F32),
            pltpu.VMEM((COLS, ROWS), F32),
            pltpu.VMEM((COLS, ROWS), F32),
            pltpu.VMEM((COLS, ROWS), F32),
            pltpu.VMEM((2, 8, ROWS), F32),
            pltpu.VMEM((2, CH, 8, ROWS), F32),
            pltpu.SemaphoreType.DMA((4,)),
            pltpu.SemaphoreType.DMA((4,)),
            pltpu.SemaphoreType.DMA((6,)),
            pltpu.SemaphoreType.DMA((6,)),
            pltpu.SemaphoreType.DMA((2,)),
            pltpu.SemaphoreType.DMA((2,)),
        ],
        compiler_params=pltpu.CompilerParams(collective_id=0, has_side_effects=True, vmem_limit_bytes=40 << 20),
    )(hidden, gating, filter_taps, upstream, norm_gain.reshape(1, COLS), *consts)


def solution(mesh):
    spec = P("ctx", "ch")
    return jax.shard_map(
        shards, mesh=mesh, in_specs=(spec, spec, spec, P("ch"), spec), out_specs=(spec,) * 4, check_vma=False
    )
```

```python
import functools
import math

import jax
import jax.numpy as jnp
import numpy as np
from jax import lax
from jax.experimental import pallas as pl
from jax.experimental.pallas import tpu as pltpu
from jax.sharding import PartitionSpec as P

MESH = pl.DeviceIdType.MESH
EPSILON = 1e-06
F32, BF16 = jnp.float32, jnp.bfloat16

WIDTH = 8192
CTX, CH = 64, 8
ROWS = 128
COLS = 1024
OWN = 16
PLANE, PLANES = 8, 8
LENGTH = CTX * ROWS
VMEM_BYTES = 56 << 20


def split(values):
    high = values.astype(BF16)
    return high, (values - high.astype(F32)).astype(BF16)


def tables():
    wave = np.arange(CTX)[:, None] + 0.25
    block = 2.0 * np.pi * wave * np.arange(CTX)[None, :] / CTX
    twist = 2.0 * np.pi * wave * np.arange(ROWS)[None, :] / LENGTH
    inner = 2.0 * np.pi * np.arange(ROWS)[:, None] * np.arange(ROWS)[None, :] / ROWS
    outer = np.concatenate([np.cos(block), -np.sin(block)], 0)
    dense = np.block([[np.cos(inner), -np.sin(inner)], [np.sin(inner), np.cos(inner)]])
    factor = 1.0 / (math.sqrt(LENGTH) * LENGTH)
    back = outer.T * factor
    twisted = np.stack([np.cos(twist), np.sin(twist)])
    return [t.astype(np.float32) for t in (outer, back, dense, dense.T, twisted)]


def dot(a, b):
    return jnp.dot(a, b, preferred_element_type=F32)


def kernel(
    hidden_hbm, gating_hbm, taps_hbm, upstream_hbm, gain_hbm, outer_hbm, back_hbm, dense_hbm, turned_hbm, twist_hbm,
    output, gate_grad, filter_grad, hidden_grad,
    hidden, gating, taps, upstream, gain_ref, outer_f32, back_f32, dense_f32, turned_f32, twist_ref,
    outer_ref, back_ref, dense_ref, turned_ref,
    send, recv, spec, part_hi, part_lo, wide, stage, hidden_t, gain_t, sums, sums_in,
    load_sem, send_sem, recv_sem, sum_send, sum_recv,
):
    me, mych = lax.axis_index("ctx"), lax.axis_index("ch")
    plane, place = me // PLANE, lax.rem(me, PLANE)
    loads = [
        pltpu.make_async_copy(src, dst, load_sem.at[i])
        for i, (src, dst) in enumerate(
            (
                (taps_hbm, taps), (hidden_hbm, hidden), (upstream_hbm, upstream), (gating_hbm, gating),
                (gain_hbm, gain_ref), (outer_hbm, outer_f32), (back_hbm, back_f32),
                (dense_hbm, dense_f32), (turned_hbm, turned_f32), (twist_hbm, twist_ref),
            )
        )
    ]
    loads[0].start()

    def far_plane(i):
        step = PLANES // 2 + jnp.where(lax.rem(i, 2) == 1, -((i + 1) // 2), i // 2)
        return lax.rem(plane + step, PLANES)

    barrier = pltpu.get_barrier_semaphore()

    def greet(peer):
        pl.semaphore_signal(barrier, inc=1, device_id={"ctx": peer}, device_id_type=MESH)

    def greet_plane(i, carry):
        for j in range(PLANE):
            greet(far_plane(i) * PLANE + j)
        return carry

    lax.fori_loop(0, PLANES - 1, greet_plane, 0)
    for i in range(1, PLANE):
        greet(plane * PLANE + lax.rem(place + i, PLANE))
    for i in range(1, CH):
        peer = lax.rem(mych + i, CH)
        pl.semaphore_signal(barrier, inc=1, device_id={"ch": peer}, device_id_type=MESH)
    for load in loads[1:]:
        load.start()

    def exchange(a, fill):
        def one(to, peer):
            pltpu.make_async_remote_copy(
                src_ref=send.at[a, peer], dst_ref=recv.at[a, me],
                send_sem=send_sem.at[a], recv_sem=recv_sem.at[a, plane],
                device_id={"ctx": peer}, device_id_type=MESH,
            ).start()

        def there(i, carry):
            to = far_plane(i)
            fill(to)
            for j in range(PLANE):
                one(to, to * PLANE + lax.rem(place + j, PLANE))
            return carry

        lax.fori_loop(0, PLANES - 1, there, 0)
        fill(plane)
        for j in range(1, PLANE):
            one(plane, plane * PLANE + lax.rem(place + j, PLANE))
        recv[a, me] = send[a, me]

    def arrivals(a, use):
        def wait(at, sem):
            pltpu.make_async_remote_copy(
                src_ref=send.at[a, at], dst_ref=recv.at[a, at], send_sem=send_sem.at[a], recv_sem=sem,
                device_id={"ctx": lax.rem(me + 1, CTX)}, device_id_type=MESH,
            ).wait_recv()

        def there(i, carry):
            source = far_plane(i)
            wait(pl.ds(source * PLANE, PLANE), recv_sem.at[a, source])
            use(source)
            return carry

        lax.fori_loop(0, PLANES - 1, there, 0)
        wait(pl.ds(0, PLANE - 1), recv_sem.at[a, plane])
        use(plane)

    def sent(a):
        rest = pl.ds(0, CTX - 1)
        pltpu.make_async_remote_copy(
            src_ref=send.at[a, rest], dst_ref=recv.at[a, rest], send_sem=send_sem.at[a], recv_sem=recv_sem.at[a, 0],
            device_id={"ctx": lax.rem(me + 1, CTX)}, device_id_type=MESH,
        ).wait_send()

    def add_up(which, partial):
        sums[which] = partial
        sums_in[which, mych] = partial

        def one(i, carry):
            peer = lax.rem(mych + i, CH)
            pltpu.make_async_remote_copy(
                src_ref=sums.at[which], dst_ref=sums_in.at[which, mych],
                send_sem=sum_send.at[which], recv_sem=sum_recv.at[which],
                device_id={"ch": peer}, device_id_type=MESH,
            ).start()
            return carry

        lax.fori_loop(1, CH, one, 0)

    def whole_sum(which):
        rest = pl.ds(0, CH - 1)
        return pltpu.make_async_remote_copy(
            src_ref=sums_in.at[which, rest], dst_ref=sums_in.at[which, rest],
            send_sem=sum_send.at[which], recv_sem=sum_recv.at[which],
            device_id={"ch": lax.rem(mych + 1, CH)}, device_id_type=MESH,
        )

    def added(which):
        whole_sum(which).wait_recv()
        total = jnp.sum(sums_in[which], axis=0)
        return jnp.sum(total, axis=0, keepdims=True) * (1.0 / WIDTH)

    def part(block):
        return pl.ds(pl.multiple_of(block * 128, 128), 128), pl.ds(block * PLANE, PLANE)

    def turn_out(a, block, values):
        send[a, part(block)[1]] = jnp.transpose(values).reshape(PLANE, OWN, ROWS).astype(BF16)

    def turn_in(a, block):
        return recv[a, part(block)[1]].astype(F32).reshape(128, ROWS)

    def to_stage(a):
        def use(block):
            stage[part(block)[0], :] = turn_in(a, block)

        return use

    def from_stage(a):
        def fill(block):
            send[a, part(block)[1]] = stage[part(block)[0], :].reshape(PLANE, OWN, ROWS).astype(BF16)

        return fill

    def forward(a):
        for p in range(OWN // 2):
            x = jnp.concatenate([stage[pl.ds(2 * p + j, CTX, stride=OWN), :].astype(BF16) for j in (0, 1)], 1)
            waves = dot(outer_ref[...], jnp.concatenate([x, x], 0))
            for j in (0, 1):
                re, im = waves[:CTX, j * ROWS : (j + 1) * ROWS], waves[CTX:, j * ROWS : (j + 1) * ROWS]
                q = jnp.concatenate(
                    [re * twist_ref[0] + im * twist_ref[1], im * twist_ref[0] - re * twist_ref[1]], 1
                )
                at = pl.ds((2 * p + j) * CTX, CTX)
                part_hi[at, :], part_lo[at, :] = split(q)
        for b in range(COLS // 256):
            at = pl.ds(b * 256, 256)
            high = part_hi[at, :]
            spec[a, at, :] = dot(high, dense_ref[0]) + (dot(high, dense_ref[1]) + dot(part_lo[at, :], dense_ref[0]))

    def inverse(first, second, conjugate):
        for b in range(COLS // 256):
            at = pl.ds(b * 256, 256)
            fr, fi = spec[first, at, :ROWS], spec[first, at, ROWS:]
            sr, si = spec[second, at, :ROWS], spec[second, at, ROWS:]
            if conjugate:
                re, im = fr * sr + fi * si, fr * si - fi * sr
            else:
                re, im = fr * sr - fi * si, fr * si + fi * sr
            high, low = split(jnp.concatenate([re, im], 1))
            wide[at, :] = dot(high, turned_ref[0]) + (dot(high, turned_ref[1]) + dot(low, turned_ref[0]))
        for p in range(OWN // 2):
            u = []
            for j in (0, 1):
                at = pl.ds((2 * p + j) * CTX, CTX)
                re, im = wide[at, :ROWS], wide[at, ROWS:]
                u.append(
                    jnp.concatenate(
                        [re * twist_ref[0] - im * twist_ref[1], re * twist_ref[1] + im * twist_ref[0]], 0
                    )
                )
            high, low = split(jnp.concatenate(u, 1))
            y = dot(back_ref[...], jnp.concatenate([high, low, high], 0))
            for j in (0, 1):
                stage[pl.ds(2 * p + j, CTX, stride=OWN), :] = y[:, j * ROWS : (j + 1) * ROWS]

    blocks = range(COLS // 128)

    loads[0].wait()
    for i in blocks:
        turn_out(0, i, taps[:, part(i)[0]].astype(F32))
    pl.semaphore_wait(barrier, CTX - 1 + CH - 1)
    exchange(0, lambda block: None)

    loads[1].wait()
    partial = jnp.zeros((8, ROWS), F32)
    for i in blocks:
        turned = jnp.transpose(hidden[:, part(i)[0]].astype(F32))
        hidden_t[part(i)[0], :] = turned
        partial = partial + jnp.sum((turned * turned).reshape(16, 8, ROWS), axis=0)
    add_up(0, partial)

    loads[2].wait()
    loads[3].wait()

    def conv_grad(block):
        at = part(block)[0]
        turn_out(1, block, upstream[:, at].astype(F32) * gating[:, at].astype(F32))

    exchange(1, conv_grad)

    loads[4].wait()
    for i in blocks:
        at = part(i)[0]
        gain_t[at, :] = jnp.transpose(jnp.broadcast_to(gain_ref[:, at], (ROWS, 128)))
    inverse_rms = lax.rsqrt(added(0) + EPSILON)

    def mixed(block):
        at, owners = part(block)
        normed = hidden_t[at, :] * inverse_rms
        hidden_t[at, :] = normed
        send[2, owners] = (normed * gain_t[at, :]).astype(BF16).reshape(PLANE, OWN, ROWS)

    exchange(2, mixed)

    for load in loads[5:]:
        load.wait()
    high, low = split(outer_f32[...])
    outer_ref[...] = jnp.concatenate([high, low], 1)
    high, low = split(back_f32[...])
    back_ref[...] = jnp.concatenate([high, high, low], 1)
    dense_ref[0], dense_ref[1] = split(dense_f32[...])
    turned_ref[0], turned_ref[1] = split(turned_f32[...])

    arrivals(0, to_stage(0))
    forward(0)
    arrivals(1, to_stage(1))
    forward(1)
    inverse(0, 1, True)
    exchange(3, from_stage(3))
    arrivals(2, to_stage(2))
    forward(2)
    inverse(2, 0, False)
    exchange(4, from_stage(4))
    inverse(2, 1, True)
    exchange(5, from_stage(5))

    sums[1] = jnp.zeros((8, ROWS), F32)

    def project(block):
        at = part(block)[0]
        scaled = turn_in(3, block) * gain_t[at, :]
        gain_t[at, :] = scaled
        sums[1] = sums[1] + jnp.sum((scaled * hidden_t[at, :]).reshape(16, 8, ROWS), axis=0)

    arrivals(3, project)
    add_up(1, sums[1])
    projection = added(1)
    for i in blocks:
        at = part(i)[0]
        value = inverse_rms * (gain_t[at, :] - hidden_t[at, :] * projection)
        hidden_grad[:, at] = jnp.transpose(value).astype(BF16)

    def gated(block):
        at = part(block)[0]
        value = jnp.transpose(turn_in(4, block))
        output[:, at] = (gating[:, at].astype(F32) * value).astype(BF16)
        gate_grad[:, at] = (upstream[:, at].astype(F32) * value).astype(BF16)

    arrivals(4, gated)

    def taps_grad(block):
        filter_grad[:, part(block)[0]] = jnp.transpose(turn_in(5, block)).astype(BF16)

    arrivals(5, taps_grad)

    for a in range(6):
        sent(a)
    for which in (0, 1):
        whole_sum(which).wait_send()


def finish(*refs):
    copies = [pltpu.make_async_copy(refs[i], refs[4 + i], refs[8].at[i]) for i in range(4)]
    for copy in copies:
        copy.start()
    for copy in copies:
        copy.wait()


def shards(hidden, gating, filter_taps, norm_gain, upstream):
    consts = [jnp.asarray(t) for t in tables()]
    vmem, hbm = pl.BlockSpec(memory_space=pltpu.VMEM), pl.BlockSpec(memory_space=pltpu.HBM)
    block = pltpu.VMEM((ROWS, COLS), BF16)
    gain = norm_gain.reshape(1, COLS)
    results = pl.pallas_call(
        kernel,
        out_shape=(pltpu.VMEM((ROWS, COLS), BF16),) * 4,
        in_specs=[hbm] * 10,
        out_specs=(vmem,) * 4,
        scratch_shapes=[block] * 4
        + [pltpu.VMEM(t.shape, t.dtype) for t in (gain, *consts)]
        + [
            pltpu.VMEM((2 * CTX, 2 * CTX), BF16),
            pltpu.VMEM((CTX, 6 * CTX), BF16),
            pltpu.VMEM((2, 2 * ROWS, 2 * ROWS), BF16),
            pltpu.VMEM((2, 2 * ROWS, 2 * ROWS), BF16),
            pltpu.VMEM((6, CTX, OWN, ROWS), BF16),
            pltpu.VMEM((6, CTX, OWN, ROWS), BF16),
            pltpu.VMEM((3, COLS, 2 * ROWS), F32),
            pltpu.VMEM((COLS, 2 * ROWS), BF16),
            pltpu.VMEM((COLS, 2 * ROWS), BF16),
            pltpu.VMEM((COLS, 2 * ROWS), F32),
            pltpu.VMEM((COLS, ROWS), F32),
            pltpu.VMEM((COLS, ROWS), F32),
            pltpu.VMEM((COLS, ROWS), F32),
            pltpu.VMEM((2, 8, ROWS), F32),
            pltpu.VMEM((2, CH, 8, ROWS), F32),
            pltpu.SemaphoreType.DMA((10,)),
            pltpu.SemaphoreType.DMA((6,)),
            pltpu.SemaphoreType.DMA((6, PLANES)),
            pltpu.SemaphoreType.DMA((2,)),
            pltpu.SemaphoreType.DMA((2,)),
        ],
        compiler_params=pltpu.CompilerParams(collective_id=0, has_side_effects=True, vmem_limit_bytes=VMEM_BYTES),
    )(hidden, gating, filter_taps, upstream, gain, *consts)
    return pl.pallas_call(
        finish,
        out_shape=(pltpu.HBM((ROWS, COLS), BF16),) * 4,
        in_specs=[vmem] * 4,
        out_specs=(hbm,) * 4,
        scratch_shapes=[pltpu.SemaphoreType.DMA((4,))],
        compiler_params=pltpu.CompilerParams(vmem_limit_bytes=1 << 20),
    )(*results)


def solution(mesh):
    spec = P("ctx", "ch")
    return jax.shard_map(
        shards, mesh=mesh, in_specs=(spec, spec, spec, P("ch"), spec), out_specs=(spec,) * 4, check_vma=False
    )
```

```python
import functools
import math

import jax
import jax.numpy as jnp
import numpy as np
from jax import lax
from jax.experimental import pallas as pl
from jax.experimental.pallas import tpu as pltpu
from jax.sharding import PartitionSpec as P

MESH = pl.DeviceIdType.MESH
EPSILON = 1e-06
F32, BF16 = jnp.float32, jnp.bfloat16

WIDTH = 8192
CTX, CH = 64, 8
ROWS = 128
COLS = 1024
OWN = 16
PLANE, PLANES = 8, 8
AGENT = 4
LENGTH = CTX * ROWS
VMEM_BYTES = 56 << 20


def split(values):
    high = values.astype(BF16)
    return high, (values - high.astype(F32)).astype(BF16)


def tables():
    wave = np.arange(CTX)[:, None] + 0.25
    block = 2.0 * np.pi * wave * np.arange(CTX)[None, :] / CTX
    twist = 2.0 * np.pi * wave * np.arange(ROWS)[None, :] / LENGTH
    inner = 2.0 * np.pi * np.arange(ROWS)[:, None] * np.arange(ROWS)[None, :] / ROWS
    outer = np.concatenate([np.cos(block), -np.sin(block)], 0)
    dense = np.block([[np.cos(inner), -np.sin(inner)], [np.sin(inner), np.cos(inner)]])
    factor = 1.0 / (math.sqrt(LENGTH) * LENGTH)
    back = outer.T * factor
    twisted = np.stack([np.cos(twist), np.sin(twist)])
    return [t.astype(np.float32) for t in (outer, back, dense, dense.T, twisted)]


def dot(a, b):
    return jnp.dot(a, b, preferred_element_type=F32)


def kernel(
    hidden_hbm, gating_hbm, taps_hbm, upstream_hbm, gain_hbm, outer_hbm, back_hbm, dense_hbm, turned_hbm, twist_hbm,
    output, gate_grad, filter_grad, hidden_grad,
    hidden, gating, taps, upstream, gain_ref, outer_f32, back_f32, dense_f32, turned_f32, twist_ref,
    outer_ref, back_ref, dense_ref, turned_ref,
    send, recv, spec, part_hi, part_lo, wide, stage, hidden_t, gain_t, sums, sums_in,
    load_sem, send_sem, recv_sem, sum_send, sum_recv, relay,
):
    me, mych = lax.axis_index("ctx"), lax.axis_index("ch")
    plane, place = me // PLANE, lax.rem(me, PLANE)
    loads = [
        pltpu.make_async_copy(src, dst, load_sem.at[i])
        for i, (src, dst) in enumerate(
            (
                (taps_hbm, taps), (hidden_hbm, hidden), (upstream_hbm, upstream), (gating_hbm, gating),
                (gain_hbm, gain_ref), (outer_hbm, outer_f32), (back_hbm, back_f32),
                (dense_hbm, dense_f32), (turned_hbm, turned_f32), (twist_hbm, twist_ref),
            )
        )
    ]
    loads[0].start()

    def far_plane(i):
        step = PLANES // 2 + jnp.where(lax.rem(i, 2) == 1, -((i + 1) // 2), i // 2)
        return lax.rem(plane + step, PLANES)

    barrier = pltpu.get_barrier_semaphore()

    def greet(peer):
        pl.semaphore_signal(barrier, inc=1, device_id={"ctx": peer}, device_id_type=MESH)

    def greet_plane(i, carry):
        for j in range(PLANE):
            greet(far_plane(i) * PLANE + j)
        return carry

    lax.fori_loop(0, PLANES - 1, greet_plane, 0)
    for i in range(1, PLANE):
        greet(plane * PLANE + lax.rem(place + i, PLANE))
    direct = plane <= AGENT

    def to_channels(semaphore):
        for i in range(1, CH):
            peer = lax.rem(mych + i, CH)
            pl.semaphore_signal(semaphore, inc=1, device_id={"ch": peer}, device_id_type=MESH)

    pl.when(direct)(lambda: to_channels(barrier))
    for load in loads[1:]:
        load.start()

    def exchange(a, fill):
        def one(to, peer):
            pltpu.make_async_remote_copy(
                src_ref=send.at[a, peer], dst_ref=recv.at[a, me],
                send_sem=send_sem.at[a], recv_sem=recv_sem.at[a, plane],
                device_id={"ctx": peer}, device_id_type=MESH,
            ).start()

        def there(i, carry):
            to = far_plane(i)
            fill(to)
            for j in range(PLANE):
                one(to, to * PLANE + lax.rem(place + j, PLANE))
            return carry

        lax.fori_loop(0, PLANES - 1, there, 0)
        fill(plane)
        for j in range(1, PLANE):
            one(plane, plane * PLANE + lax.rem(place + j, PLANE))
        recv[a, me] = send[a, me]

    def arrivals(a, use):
        def wait(at, sem):
            pltpu.make_async_remote_copy(
                src_ref=send.at[a, at], dst_ref=recv.at[a, at], send_sem=send_sem.at[a], recv_sem=sem,
                device_id={"ctx": lax.rem(me + 1, CTX)}, device_id_type=MESH,
            ).wait_recv()

        def there(i, carry):
            source = far_plane(i)
            wait(pl.ds(source * PLANE, PLANE), recv_sem.at[a, source])
            use(source)
            return carry

        lax.fori_loop(0, PLANES - 1, there, 0)
        wait(pl.ds(0, PLANE - 1), recv_sem.at[a, plane])
        use(plane)

    def sent(a):
        rest = pl.ds(0, CTX - 1)
        pltpu.make_async_remote_copy(
            src_ref=send.at[a, rest], dst_ref=recv.at[a, rest], send_sem=send_sem.at[a], recv_sem=recv_sem.at[a, 0],
            device_id={"ctx": lax.rem(me + 1, CTX)}, device_id_type=MESH,
        ).wait_send()

    def add_up(which, partial):
        sums[which] = partial
        sums_in[which, mych] = partial

        def one(i, carry):
            peer = lax.rem(mych + i, CH)
            pltpu.make_async_remote_copy(
                src_ref=sums.at[which], dst_ref=sums_in.at[which, mych],
                send_sem=sum_send.at[which], recv_sem=sum_recv.at[which],
                device_id={"ch": peer}, device_id_type=MESH,
            ).start()
            return carry

        lax.fori_loop(1, CH, one, 0)

    def whole_sum(which):
        rest = pl.ds(0, CH - 1)
        return pltpu.make_async_remote_copy(
            src_ref=sums_in.at[which, rest], dst_ref=sums_in.at[which, rest],
            send_sem=sum_send.at[which], recv_sem=sum_recv.at[which],
            device_id={"ch": lax.rem(mych + 1, CH)}, device_id_type=MESH,
        )

    def added(which):
        whole_sum(which).wait_recv()
        total = jnp.sum(sums_in[which], axis=0)
        return jnp.sum(total, axis=0, keepdims=True) * (1.0 / WIDTH)

    def part(block):
        return pl.ds(pl.multiple_of(block * 128, 128), 128), pl.ds(block * PLANE, PLANE)

    def turn_out(a, block, values):
        send[a, part(block)[1]] = jnp.transpose(values).reshape(PLANE, OWN, ROWS).astype(BF16)

    def turn_in(a, block):
        return recv[a, part(block)[1]].astype(F32).reshape(128, ROWS)

    def to_stage(a):
        def use(block):
            stage[part(block)[0], :] = turn_in(a, block)

        return use

    def from_stage(a):
        def fill(block):
            send[a, part(block)[1]] = stage[part(block)[0], :].reshape(PLANE, OWN, ROWS).astype(BF16)

        return fill

    def forward(a):
        for p in range(OWN // 2):
            x = jnp.concatenate([stage[pl.ds(2 * p + j, CTX, stride=OWN), :].astype(BF16) for j in (0, 1)], 1)
            waves = dot(outer_ref[...], jnp.concatenate([x, x], 0))
            for j in (0, 1):
                re, im = waves[:CTX, j * ROWS : (j + 1) * ROWS], waves[CTX:, j * ROWS : (j + 1) * ROWS]
                q = jnp.concatenate(
                    [re * twist_ref[0] + im * twist_ref[1], im * twist_ref[0] - re * twist_ref[1]], 1
                )
                at = pl.ds((2 * p + j) * CTX, CTX)
                part_hi[at, :], part_lo[at, :] = split(q)
        for b in range(COLS // 256):
            at = pl.ds(b * 256, 256)
            high = part_hi[at, :]
            spec[a, at, :] = dot(high, dense_ref[0]) + (dot(high, dense_ref[1]) + dot(part_lo[at, :], dense_ref[0]))

    def inverse(first, second, conjugate):
        for b in range(COLS // 256):
            at = pl.ds(b * 256, 256)
            fr, fi = spec[first, at, :ROWS], spec[first, at, ROWS:]
            sr, si = spec[second, at, :ROWS], spec[second, at, ROWS:]
            if conjugate:
                re, im = fr * sr + fi * si, fr * si - fi * sr
            else:
                re, im = fr * sr - fi * si, fr * si + fi * sr
            high, low = split(jnp.concatenate([re, im], 1))
            wide[at, :] = dot(high, turned_ref[0]) + (dot(high, turned_ref[1]) + dot(low, turned_ref[0]))
        for p in range(OWN // 2):
            u = []
            for j in (0, 1):
                at = pl.ds((2 * p + j) * CTX, CTX)
                re, im = wide[at, :ROWS], wide[at, ROWS:]
                u.append(
                    jnp.concatenate(
                        [re * twist_ref[0] - im * twist_ref[1], re * twist_ref[1] + im * twist_ref[0]], 0
                    )
                )
            high, low = split(jnp.concatenate(u, 1))
            y = dot(back_ref[...], jnp.concatenate([high, low, high], 0))
            for j in (0, 1):
                stage[pl.ds(2 * p + j, CTX, stride=OWN), :] = y[:, j * ROWS : (j + 1) * ROWS]

    blocks = range(COLS // 128)

    loads[0].wait()
    for i in blocks:
        turn_out(0, i, taps[:, part(i)[0]].astype(F32))
    loads[1].wait()
    partial = jnp.zeros((8, ROWS), F32)
    for i in blocks:
        turned = jnp.transpose(hidden[:, part(i)[0]].astype(F32))
        hidden_t[part(i)[0], :] = turned
        partial = partial + jnp.sum((turned * turned).reshape(16, 8, ROWS), axis=0)

    @pl.when(direct)
    def _():
        pl.semaphore_wait(barrier, CTX - 1 + CH - 1)
        add_up(0, partial)

    @pl.when(plane > AGENT)
    def _():
        pl.semaphore_wait(barrier, CTX - 1)
        agent = AGENT * PLANE + place
        pl.semaphore_signal(relay.at[0], inc=1, device_id={"ctx": agent}, device_id_type=MESH)

    exchange(0, lambda block: None)

    @pl.when(plane == AGENT)
    def _():
        pl.semaphore_wait(relay.at[0], PLANES - 1 - AGENT)
        to_channels(relay.at[1])

    @pl.when(plane > AGENT)
    def _():
        pl.semaphore_wait(relay.at[2], 1)
        add_up(0, partial)

    loads[2].wait()
    loads[3].wait()

    def conv_grad(block):
        at = part(block)[0]
        turn_out(1, block, upstream[:, at].astype(F32) * gating[:, at].astype(F32))

    exchange(1, conv_grad)

    @pl.when(plane == AGENT)
    def _():
        pl.semaphore_wait(relay.at[1], CH - 1)
        for later in range(AGENT + 1, PLANES):
            peer = later * PLANE + place
            pl.semaphore_signal(relay.at[2], inc=1, device_id={"ctx": peer}, device_id_type=MESH)

    loads[4].wait()
    for i in blocks:
        at = part(i)[0]
        gain_t[at, :] = jnp.transpose(jnp.broadcast_to(gain_ref[:, at], (ROWS, 128)))
    inverse_rms = lax.rsqrt(added(0) + EPSILON)

    def mixed(block):
        at, owners = part(block)
        normed = hidden_t[at, :] * inverse_rms
        hidden_t[at, :] = normed
        send[2, owners] = (normed * gain_t[at, :]).astype(BF16).reshape(PLANE, OWN, ROWS)

    exchange(2, mixed)

    for load in loads[5:]:
        load.wait()
    high, low = split(outer_f32[...])
    outer_ref[...] = jnp.concatenate([high, low], 1)
    high, low = split(back_f32[...])
    back_ref[...] = jnp.concatenate([high, high, low], 1)
    dense_ref[0], dense_ref[1] = split(dense_f32[...])
    turned_ref[0], turned_ref[1] = split(turned_f32[...])

    arrivals(0, to_stage(0))
    forward(0)
    arrivals(1, to_stage(1))
    forward(1)
    inverse(0, 1, True)
    exchange(3, from_stage(3))
    arrivals(2, to_stage(2))
    forward(2)
    inverse(2, 0, False)
    exchange(4, from_stage(4))
    inverse(2, 1, True)

    sums[1] = jnp.zeros((8, ROWS), F32)

    def project(block):
        at = part(block)[0]
        scaled = turn_in(3, block) * gain_t[at, :]
        gain_t[at, :] = scaled
        sums[1] = sums[1] + jnp.sum((scaled * hidden_t[at, :]).reshape(16, 8, ROWS), axis=0)

    arrivals(3, project)
    add_up(1, sums[1])
    exchange(5, from_stage(5))

    def gated(block):
        at = part(block)[0]
        value = jnp.transpose(turn_in(4, block))
        output[:, at] = (gating[:, at].astype(F32) * value).astype(BF16)
        gate_grad[:, at] = (upstream[:, at].astype(F32) * value).astype(BF16)

    arrivals(4, gated)
    projection = added(1)
    for i in blocks:
        at = part(i)[0]
        value = inverse_rms * (gain_t[at, :] - hidden_t[at, :] * projection)
        hidden_grad[:, at] = jnp.transpose(value).astype(BF16)

    def taps_grad(block):
        filter_grad[:, part(block)[0]] = jnp.transpose(turn_in(5, block)).astype(BF16)

    arrivals(5, taps_grad)

    for a in range(6):
        sent(a)
    for which in (0, 1):
        whole_sum(which).wait_send()


def finish(*refs):
    copies = [pltpu.make_async_copy(refs[i], refs[4 + i], refs[8].at[i]) for i in range(4)]
    for copy in copies:
        copy.start()
    for copy in copies:
        copy.wait()


def shards(hidden, gating, filter_taps, norm_gain, upstream):
    consts = [jnp.asarray(t) for t in tables()]
    vmem, hbm = pl.BlockSpec(memory_space=pltpu.VMEM), pl.BlockSpec(memory_space=pltpu.HBM)
    block = pltpu.VMEM((ROWS, COLS), BF16)
    gain = norm_gain.reshape(1, COLS)
    results = pl.pallas_call(
        kernel,
        out_shape=(pltpu.VMEM((ROWS, COLS), BF16),) * 4,
        in_specs=[hbm] * 10,
        out_specs=(vmem,) * 4,
        scratch_shapes=[block] * 4
        + [pltpu.VMEM(t.shape, t.dtype) for t in (gain, *consts)]
        + [
            pltpu.VMEM((2 * CTX, 2 * CTX), BF16),
            pltpu.VMEM((CTX, 6 * CTX), BF16),
            pltpu.VMEM((2, 2 * ROWS, 2 * ROWS), BF16),
            pltpu.VMEM((2, 2 * ROWS, 2 * ROWS), BF16),
            pltpu.VMEM((6, CTX, OWN, ROWS), BF16),
            pltpu.VMEM((6, CTX, OWN, ROWS), BF16),
            pltpu.VMEM((3, COLS, 2 * ROWS), F32),
            pltpu.VMEM((COLS, 2 * ROWS), BF16),
            pltpu.VMEM((COLS, 2 * ROWS), BF16),
            pltpu.VMEM((COLS, 2 * ROWS), F32),
            pltpu.VMEM((COLS, ROWS), F32),
            pltpu.VMEM((COLS, ROWS), F32),
            pltpu.VMEM((COLS, ROWS), F32),
            pltpu.VMEM((2, 8, ROWS), F32),
            pltpu.VMEM((2, CH, 8, ROWS), F32),
            pltpu.SemaphoreType.DMA((10,)),
            pltpu.SemaphoreType.DMA((6,)),
            pltpu.SemaphoreType.DMA((6, PLANES)),
            pltpu.SemaphoreType.DMA((2,)),
            pltpu.SemaphoreType.DMA((2,)),
            pltpu.SemaphoreType.REGULAR((3,)),
        ],
        compiler_params=pltpu.CompilerParams(collective_id=0, has_side_effects=True, vmem_limit_bytes=VMEM_BYTES),
    )(hidden, gating, filter_taps, upstream, gain, *consts)
    return pl.pallas_call(
        finish,
        out_shape=(pltpu.HBM((ROWS, COLS), BF16),) * 4,
        in_specs=[vmem] * 4,
        out_specs=(hbm,) * 4,
        scratch_shapes=[pltpu.SemaphoreType.DMA((4,))],
        compiler_params=pltpu.CompilerParams(vmem_limit_bytes=1 << 20),
    )(*results)


def solution(mesh):
    spec = P("ctx", "ch")
    return jax.shard_map(
        shards, mesh=mesh, in_specs=(spec, spec, spec, P("ch"), spec), out_specs=(spec,) * 4, check_vma=False
    )
```

```python
import functools
import math

import jax
import jax.numpy as jnp
import numpy as np
from jax import lax
from jax.experimental import pallas as pl
from jax.experimental.pallas import tpu as pltpu
from jax.sharding import PartitionSpec as P

MESH = pl.DeviceIdType.MESH
EPSILON = 1e-06
F32, BF16 = jnp.float32, jnp.bfloat16

WIDTH = 8192
CTX, CH = 64, 8
ROWS = 128
COLS = 1024
OWN = 16
PLANE, PLANES = 8, 8
AGENT = 4
LENGTH = CTX * ROWS
VMEM_BYTES = 56 << 20


def split(values):
    high = values.astype(BF16)
    return high, (values - high.astype(F32)).astype(BF16)


def tables():
    wave = np.arange(CTX)[:, None] + 0.25
    block = 2.0 * np.pi * wave * np.arange(CTX)[None, :] / CTX
    twist = 2.0 * np.pi * wave * np.arange(ROWS)[None, :] / LENGTH
    inner = 2.0 * np.pi * np.arange(ROWS)[:, None] * np.arange(ROWS)[None, :] / ROWS
    outer = np.concatenate([np.cos(block), -np.sin(block)], 0)
    dense = np.block([[np.cos(inner), -np.sin(inner)], [np.sin(inner), np.cos(inner)]])
    factor = 1.0 / (math.sqrt(LENGTH) * LENGTH)
    back = outer.T * factor
    twisted = np.stack([np.cos(twist), np.sin(twist)])
    return [t.astype(np.float32) for t in (outer, back, dense, dense.T, twisted)]


def dot(a, b):
    return jnp.dot(a, b, preferred_element_type=F32)


def kernel(
    hidden_hbm, gating_hbm, taps_hbm, upstream_hbm, gain_hbm, outer_hbm, back_hbm, dense_hbm, turned_hbm, twist_hbm,
    output, gate_grad, filter_grad, hidden_grad,
    hidden, gating, taps, upstream, gain_ref, outer_f32, back_f32, dense_f32, turned_f32, twist_ref,
    outer_ref, back_ref, dense_ref, turned_ref,
    send, recv, spec, part_hi, part_lo, wide, stage, hidden_t, gain_t, sums, sums_in,
    load_sem, send_sem, recv_sem, sum_send, sum_recv, relay,
):
    me, mych = lax.axis_index("ctx"), lax.axis_index("ch")
    plane, place = me // PLANE, lax.rem(me, PLANE)
    loads = [
        pltpu.make_async_copy(src, dst, load_sem.at[i])
        for i, (src, dst) in enumerate(
            (
                (taps_hbm, taps), (hidden_hbm, hidden), (upstream_hbm, upstream), (gating_hbm, gating),
                (gain_hbm, gain_ref), (outer_hbm, outer_f32), (back_hbm, back_f32),
                (dense_hbm, dense_f32), (turned_hbm, turned_f32), (twist_hbm, twist_ref),
            )
        )
    ]
    loads[0].start()

    def far_plane(i):
        step = PLANES // 2 + jnp.where(lax.rem(i, 2) == 1, -((i + 1) // 2), i // 2)
        return lax.rem(plane + step, PLANES)

    barrier = pltpu.get_barrier_semaphore()

    def greet(peer):
        pl.semaphore_signal(barrier, inc=1, device_id={"ctx": peer}, device_id_type=MESH)

    def greet_plane(i, carry):
        for j in range(PLANE):
            greet(far_plane(i) * PLANE + j)
        return carry

    lax.fori_loop(0, PLANES - 1, greet_plane, 0)
    for i in range(1, PLANE):
        greet(plane * PLANE + lax.rem(place + i, PLANE))
    direct = plane <= AGENT

    def to_channels(semaphore):
        for i in range(1, CH):
            peer = lax.rem(mych + i, CH)
            pl.semaphore_signal(semaphore, inc=1, device_id={"ch": peer}, device_id_type=MESH)

    pl.when(direct)(lambda: to_channels(barrier))
    for load in loads[1:]:
        load.start()

    def exchange(a, fill):
        def one(to, peer):
            pltpu.make_async_remote_copy(
                src_ref=send.at[a, peer], dst_ref=recv.at[a, me],
                send_sem=send_sem.at[a], recv_sem=recv_sem.at[a, plane],
                device_id={"ctx": peer}, device_id_type=MESH,
            ).start()

        def there(i, carry):
            to = far_plane(i)
            fill(to)
            for j in range(PLANE):
                one(to, to * PLANE + lax.rem(place + j, PLANE))
            return carry

        lax.fori_loop(0, PLANES - 1, there, 0)
        fill(plane)
        for j in range(1, PLANE):
            one(plane, plane * PLANE + lax.rem(place + j, PLANE))
        recv[a, me] = send[a, me]

    def arrivals(a, use):
        def wait(at, sem):
            pltpu.make_async_remote_copy(
                src_ref=send.at[a, at], dst_ref=recv.at[a, at], send_sem=send_sem.at[a], recv_sem=sem,
                device_id={"ctx": lax.rem(me + 1, CTX)}, device_id_type=MESH,
            ).wait_recv()

        def there(i, carry):
            source = far_plane(i)
            wait(pl.ds(source * PLANE, PLANE), recv_sem.at[a, source])
            use(source)
            return carry

        lax.fori_loop(0, PLANES - 1, there, 0)
        wait(pl.ds(0, PLANE - 1), recv_sem.at[a, plane])
        use(plane)

    def sent(a):
        rest = pl.ds(0, CTX - 1)
        pltpu.make_async_remote_copy(
            src_ref=send.at[a, rest], dst_ref=recv.at[a, rest], send_sem=send_sem.at[a], recv_sem=recv_sem.at[a, 0],
            device_id={"ctx": lax.rem(me + 1, CTX)}, device_id_type=MESH,
        ).wait_send()

    def add_up(which):
        sums_in[which, mych] = sums[which]

        def one(i, carry):
            peer = lax.rem(mych + i, CH)
            pltpu.make_async_remote_copy(
                src_ref=sums.at[which], dst_ref=sums_in.at[which, mych],
                send_sem=sum_send.at[which], recv_sem=sum_recv.at[which],
                device_id={"ch": peer}, device_id_type=MESH,
            ).start()
            return carry

        lax.fori_loop(1, CH, one, 0)

    def whole_sum(which):
        rest = pl.ds(0, CH - 1)
        return pltpu.make_async_remote_copy(
            src_ref=sums_in.at[which, rest], dst_ref=sums_in.at[which, rest],
            send_sem=sum_send.at[which], recv_sem=sum_recv.at[which],
            device_id={"ch": lax.rem(mych + 1, CH)}, device_id_type=MESH,
        )

    def added(which):
        whole_sum(which).wait_recv()
        total = jnp.sum(sums_in[which], axis=0)
        return jnp.sum(total, axis=0, keepdims=True) * (1.0 / WIDTH)

    def part(block):
        return pl.ds(pl.multiple_of(block * 128, 128), 128), pl.ds(block * PLANE, PLANE)

    def turn_out(a, block, values):
        send[a, part(block)[1]] = jnp.transpose(values).reshape(PLANE, OWN, ROWS).astype(BF16)

    def turn_in(a, block):
        return recv[a, part(block)[1]].astype(F32).reshape(128, ROWS)

    def to_stage(a):
        def use(block):
            stage[part(block)[0], :] = turn_in(a, block)

        return use

    def from_stage(a):
        def fill(block):
            send[a, part(block)[1]] = stage[part(block)[0], :].reshape(PLANE, OWN, ROWS).astype(BF16)

        return fill

    def forward(a):
        for p in range(OWN // 2):
            x = jnp.concatenate([stage[pl.ds(2 * p + j, CTX, stride=OWN), :].astype(BF16) for j in (0, 1)], 1)
            waves = dot(outer_ref[...], jnp.concatenate([x, x], 0))
            for j in (0, 1):
                re, im = waves[:CTX, j * ROWS : (j + 1) * ROWS], waves[CTX:, j * ROWS : (j + 1) * ROWS]
                q = jnp.concatenate(
                    [re * twist_ref[0] + im * twist_ref[1], im * twist_ref[0] - re * twist_ref[1]], 1
                )
                at = pl.ds((2 * p + j) * CTX, CTX)
                part_hi[at, :], part_lo[at, :] = split(q)
        for b in range(COLS // 256):
            at = pl.ds(b * 256, 256)
            high = part_hi[at, :]
            spec[a, at, :] = dot(high, dense_ref[0]) + (dot(high, dense_ref[1]) + dot(part_lo[at, :], dense_ref[0]))

    def inverse(first, second, conjugate):
        for b in range(COLS // 256):
            at = pl.ds(b * 256, 256)
            fr, fi = spec[first, at, :ROWS], spec[first, at, ROWS:]
            sr, si = spec[second, at, :ROWS], spec[second, at, ROWS:]
            if conjugate:
                re, im = fr * sr + fi * si, fr * si - fi * sr
            else:
                re, im = fr * sr - fi * si, fr * si + fi * sr
            high, low = split(jnp.concatenate([re, im], 1))
            wide[at, :] = dot(high, turned_ref[0]) + (dot(high, turned_ref[1]) + dot(low, turned_ref[0]))
        for p in range(OWN // 2):
            u = []
            for j in (0, 1):
                at = pl.ds((2 * p + j) * CTX, CTX)
                re, im = wide[at, :ROWS], wide[at, ROWS:]
                u.append(
                    jnp.concatenate(
                        [re * twist_ref[0] - im * twist_ref[1], re * twist_ref[1] + im * twist_ref[0]], 0
                    )
                )
            high, low = split(jnp.concatenate(u, 1))
            y = dot(back_ref[...], jnp.concatenate([high, low, high], 0))
            for j in (0, 1):
                stage[pl.ds(2 * p + j, CTX, stride=OWN), :] = y[:, j * ROWS : (j + 1) * ROWS]

    blocks = range(COLS // 128)

    def turn_filter():
        loads[0].wait()
        for i in blocks:
            turn_out(0, i, taps[:, part(i)[0]].astype(F32))

    def squares():
        loads[1].wait()
        partial = jnp.zeros((8, ROWS), F32)
        for i in blocks:
            turned = jnp.transpose(hidden[:, part(i)[0]].astype(F32))
            hidden_t[part(i)[0], :] = turned
            partial = partial + jnp.sum((turned * turned).reshape(16, 8, ROWS), axis=0)
        sums[0] = partial

    @pl.when(direct)
    def _():
        turn_filter()
        squares()
        pl.semaphore_wait(barrier, CTX - 1 + CH - 1)
        add_up(0)

    @pl.when(plane > AGENT)
    def _():
        pl.semaphore_wait(barrier, CTX - 1)
        agent = AGENT * PLANE + place
        pl.semaphore_signal(relay.at[0], inc=1, device_id={"ctx": agent}, device_id_type=MESH)
        turn_filter()

    exchange(0, lambda block: None)

    @pl.when(plane == AGENT)
    def _():
        pl.semaphore_wait(relay.at[0], PLANES - 1 - AGENT)
        to_channels(relay.at[1])

    @pl.when(plane > AGENT)
    def _():
        squares()
        pl.semaphore_wait(relay.at[2], 1)
        add_up(0)

    loads[2].wait()
    loads[3].wait()

    def conv_grad(block):
        at = part(block)[0]
        turn_out(1, block, upstream[:, at].astype(F32) * gating[:, at].astype(F32))

    exchange(1, conv_grad)

    @pl.when(plane == AGENT)
    def _():
        pl.semaphore_wait(relay.at[1], CH - 1)
        for later in range(AGENT + 1, PLANES):
            peer = later * PLANE + place
            pl.semaphore_signal(relay.at[2], inc=1, device_id={"ctx": peer}, device_id_type=MESH)

    loads[4].wait()
    for i in blocks:
        at = part(i)[0]
        gain_t[at, :] = jnp.transpose(jnp.broadcast_to(gain_ref[:, at], (ROWS, 128)))
    inverse_rms = lax.rsqrt(added(0) + EPSILON)

    def mixed(block):
        at, owners = part(block)
        normed = hidden_t[at, :] * inverse_rms
        hidden_t[at, :] = normed
        send[2, owners] = (normed * gain_t[at, :]).astype(BF16).reshape(PLANE, OWN, ROWS)

    exchange(2, mixed)

    for load in loads[5:]:
        load.wait()
    high, low = split(outer_f32[...])
    outer_ref[...] = jnp.concatenate([high, low], 1)
    high, low = split(back_f32[...])
    back_ref[...] = jnp.concatenate([high, high, low], 1)
    dense_ref[0], dense_ref[1] = split(dense_f32[...])
    turned_ref[0], turned_ref[1] = split(turned_f32[...])

    arrivals(0, to_stage(0))
    forward(0)
    arrivals(1, to_stage(1))
    forward(1)
    inverse(0, 1, True)
    exchange(3, from_stage(3))
    arrivals(2, to_stage(2))
    forward(2)
    inverse(2, 0, False)
    exchange(4, from_stage(4))
    inverse(2, 1, True)

    sums[1] = jnp.zeros((8, ROWS), F32)

    def project(block):
        at = part(block)[0]
        scaled = turn_in(3, block) * gain_t[at, :]
        gain_t[at, :] = scaled
        sums[1] = sums[1] + jnp.sum((scaled * hidden_t[at, :]).reshape(16, 8, ROWS), axis=0)

    arrivals(3, project)
    add_up(1)
    exchange(5, from_stage(5))

    def gated(block):
        at = part(block)[0]
        value = jnp.transpose(turn_in(4, block))
        output[:, at] = (gating[:, at].astype(F32) * value).astype(BF16)
        gate_grad[:, at] = (upstream[:, at].astype(F32) * value).astype(BF16)

    arrivals(4, gated)
    projection = added(1)
    for i in blocks:
        at = part(i)[0]
        value = inverse_rms * (gain_t[at, :] - hidden_t[at, :] * projection)
        hidden_grad[:, at] = jnp.transpose(value).astype(BF16)

    def taps_grad(block):
        filter_grad[:, part(block)[0]] = jnp.transpose(turn_in(5, block)).astype(BF16)

    arrivals(5, taps_grad)

    for a in range(6):
        sent(a)
    for which in (0, 1):
        whole_sum(which).wait_send()


def finish(*refs):
    copies = [pltpu.make_async_copy(refs[i], refs[4 + i], refs[8].at[i]) for i in range(4)]
    for copy in copies:
        copy.start()
    for copy in copies:
        copy.wait()


def shards(hidden, gating, filter_taps, norm_gain, upstream):
    consts = [jnp.asarray(t) for t in tables()]
    vmem, hbm = pl.BlockSpec(memory_space=pltpu.VMEM), pl.BlockSpec(memory_space=pltpu.HBM)
    block = pltpu.VMEM((ROWS, COLS), BF16)
    gain = norm_gain.reshape(1, COLS)
    results = pl.pallas_call(
        kernel,
        out_shape=(pltpu.VMEM((ROWS, COLS), BF16),) * 4,
        in_specs=[hbm] * 10,
        out_specs=(vmem,) * 4,
        scratch_shapes=[block] * 4
        + [pltpu.VMEM(t.shape, t.dtype) for t in (gain, *consts)]
        + [
            pltpu.VMEM((2 * CTX, 2 * CTX), BF16),
            pltpu.VMEM((CTX, 6 * CTX), BF16),
            pltpu.VMEM((2, 2 * ROWS, 2 * ROWS), BF16),
            pltpu.VMEM((2, 2 * ROWS, 2 * ROWS), BF16),
            pltpu.VMEM((6, CTX, OWN, ROWS), BF16),
            pltpu.VMEM((6, CTX, OWN, ROWS), BF16),
            pltpu.VMEM((3, COLS, 2 * ROWS), F32),
            pltpu.VMEM((COLS, 2 * ROWS), BF16),
            pltpu.VMEM((COLS, 2 * ROWS), BF16),
            pltpu.VMEM((COLS, 2 * ROWS), F32),
            pltpu.VMEM((COLS, ROWS), F32),
            pltpu.VMEM((COLS, ROWS), F32),
            pltpu.VMEM((COLS, ROWS), F32),
            pltpu.VMEM((2, 8, ROWS), F32),
            pltpu.VMEM((2, CH, 8, ROWS), F32),
            pltpu.SemaphoreType.DMA((10,)),
            pltpu.SemaphoreType.DMA((6,)),
            pltpu.SemaphoreType.DMA((6, PLANES)),
            pltpu.SemaphoreType.DMA((2,)),
            pltpu.SemaphoreType.DMA((2,)),
            pltpu.SemaphoreType.REGULAR((3,)),
        ],
        compiler_params=pltpu.CompilerParams(collective_id=0, has_side_effects=True, vmem_limit_bytes=VMEM_BYTES),
    )(hidden, gating, filter_taps, upstream, gain, *consts)
    return pl.pallas_call(
        finish,
        out_shape=(pltpu.HBM((ROWS, COLS), BF16),) * 4,
        in_specs=[vmem] * 4,
        out_specs=(hbm,) * 4,
        scratch_shapes=[pltpu.SemaphoreType.DMA((4,))],
        compiler_params=pltpu.CompilerParams(vmem_limit_bytes=1 << 20),
    )(*results)


def solution(mesh):
    spec = P("ctx", "ch")
    return jax.shard_map(
        shards, mesh=mesh, in_specs=(spec, spec, spec, P("ch"), spec), out_specs=(spec,) * 4, check_vma=False
    )
```

```python
import functools
import math

import jax
import jax.numpy as jnp
import numpy as np
from jax import lax
from jax.experimental import pallas as pl
from jax.experimental.pallas import tpu as pltpu
from jax.sharding import PartitionSpec as P

MESH = pl.DeviceIdType.MESH
EPSILON = 1e-06
F32, BF16 = jnp.float32, jnp.bfloat16

WIDTH = 8192
CTX, CH = 64, 8
ROWS = 128
COLS = 1024
OWN = 16
PLANE, PLANES = 8, 8
AGENT = 4
LENGTH = CTX * ROWS
VMEM_BYTES = 56 << 20


def split(values):
    high = values.astype(BF16)
    return high, (values - high.astype(F32)).astype(BF16)


def tables():
    wave = np.arange(CTX)[:, None] + 0.25
    block = 2.0 * np.pi * wave * np.arange(CTX)[None, :] / CTX
    twist = 2.0 * np.pi * wave * np.arange(ROWS)[None, :] / LENGTH
    inner = 2.0 * np.pi * np.arange(ROWS)[:, None] * np.arange(ROWS)[None, :] / ROWS
    outer = np.concatenate([np.cos(block), -np.sin(block)], 0)
    dense = np.block([[np.cos(inner), -np.sin(inner)], [np.sin(inner), np.cos(inner)]])
    factor = 1.0 / (math.sqrt(LENGTH) * LENGTH)
    back = outer.T * factor
    twisted = np.stack([np.cos(twist), np.sin(twist)])
    return [t.astype(np.float32) for t in (outer, back, dense, dense.T, twisted)]


def dot(a, b):
    return jnp.dot(a, b, preferred_element_type=F32)


def kernel(
    hidden_hbm, gating_hbm, taps_hbm, upstream_hbm, gain_hbm, outer_hbm, back_hbm, dense_hbm, turned_hbm, twist_hbm,
    output, gate_grad, filter_grad, hidden_grad,
    hidden, gating, taps, upstream, gain_ref, outer_f32, back_f32, dense_f32, turned_f32, twist_ref,
    outer_ref, back_ref, dense_ref, turned_ref,
    send, recv, spec, part_hi, part_lo, wide, stage, hidden_t, gain_t, sums, sums_in,
    load_sem, send_sem, recv_sem, sum_send, sum_recv, relay,
):
    me, mych = lax.axis_index("ctx"), lax.axis_index("ch")
    plane, place = me // PLANE, lax.rem(me, PLANE)
    loads = [
        pltpu.make_async_copy(src, dst, load_sem.at[i])
        for i, (src, dst) in enumerate(
            (
                (taps_hbm, taps), (hidden_hbm, hidden), (upstream_hbm, upstream), (gating_hbm, gating),
                (gain_hbm, gain_ref), (outer_hbm, outer_f32), (back_hbm, back_f32),
                (dense_hbm, dense_f32), (turned_hbm, turned_f32), (twist_hbm, twist_ref),
            )
        )
    ]
    loads[0].start()

    def far_plane(i):
        step = PLANES // 2 + jnp.where(lax.rem(i, 2) == 1, -((i + 1) // 2), i // 2)
        return lax.rem(plane + step, PLANES)

    barrier = pltpu.get_barrier_semaphore()

    def greet(peer):
        pl.semaphore_signal(barrier, inc=1, device_id={"ctx": peer}, device_id_type=MESH)

    def greet_plane(i, carry):
        for j in range(PLANE):
            greet(far_plane(i) * PLANE + j)
        return carry

    lax.fori_loop(0, PLANES - 1, greet_plane, 0)
    for i in range(1, PLANE):
        greet(plane * PLANE + lax.rem(place + i, PLANE))
    direct = plane <= AGENT

    def to_channels(semaphore):
        for i in range(1, CH):
            peer = lax.rem(mych + i, CH)
            pl.semaphore_signal(semaphore, inc=1, device_id={"ch": peer}, device_id_type=MESH)

    pl.when(direct)(lambda: to_channels(barrier))
    for load in loads[1:]:
        load.start()

    def exchange(a, fill):
        def one(to, peer):
            pltpu.make_async_remote_copy(
                src_ref=send.at[a, peer], dst_ref=recv.at[a, me],
                send_sem=send_sem.at[a], recv_sem=recv_sem.at[a, plane],
                device_id={"ctx": peer}, device_id_type=MESH,
            ).start()

        def there(i, carry):
            to = far_plane(i)
            fill(to)
            for j in range(PLANE):
                one(to, to * PLANE + lax.rem(place + j, PLANE))
            return carry

        lax.fori_loop(0, PLANES - 1, there, 0)
        fill(plane)
        for j in range(1, PLANE):
            one(plane, plane * PLANE + lax.rem(place + j, PLANE))
        recv[a, me] = send[a, me]

    def arrivals(a, use):
        def wait(at, sem):
            pltpu.make_async_remote_copy(
                src_ref=send.at[a, at], dst_ref=recv.at[a, at], send_sem=send_sem.at[a], recv_sem=sem,
                device_id={"ctx": lax.rem(me + 1, CTX)}, device_id_type=MESH,
            ).wait_recv()

        def there(i, carry):
            source = far_plane(i)
            wait(pl.ds(source * PLANE, PLANE), recv_sem.at[a, source])
            use(source)
            return carry

        lax.fori_loop(0, PLANES - 1, there, 0)
        wait(pl.ds(0, PLANE - 1), recv_sem.at[a, plane])
        use(plane)

    def sent(a):
        rest = pl.ds(0, CTX - 1)
        pltpu.make_async_remote_copy(
            src_ref=send.at[a, rest], dst_ref=recv.at[a, rest], send_sem=send_sem.at[a], recv_sem=recv_sem.at[a, 0],
            device_id={"ctx": lax.rem(me + 1, CTX)}, device_id_type=MESH,
        ).wait_send()

    def add_up(which):
        sums_in[which, mych] = sums[which]

        def one(i, carry):
            peer = lax.rem(mych + i, CH)
            pltpu.make_async_remote_copy(
                src_ref=sums.at[which], dst_ref=sums_in.at[which, mych],
                send_sem=sum_send.at[which], recv_sem=sum_recv.at[which],
                device_id={"ch": peer}, device_id_type=MESH,
            ).start()
            return carry

        lax.fori_loop(1, CH, one, 0)

    def whole_sum(which):
        rest = pl.ds(0, CH - 1)
        return pltpu.make_async_remote_copy(
            src_ref=sums_in.at[which, rest], dst_ref=sums_in.at[which, rest],
            send_sem=sum_send.at[which], recv_sem=sum_recv.at[which],
            device_id={"ch": lax.rem(mych + 1, CH)}, device_id_type=MESH,
        )

    def added(which):
        whole_sum(which).wait_recv()
        total = jnp.sum(sums_in[which], axis=0)
        return jnp.sum(total, axis=0, keepdims=True) * (1.0 / WIDTH)

    def part(block):
        return pl.ds(pl.multiple_of(block * 128, 128), 128), pl.ds(block * PLANE, PLANE)

    def turn_out(a, block, values):
        send[a, part(block)[1]] = jnp.transpose(values).reshape(PLANE, OWN, ROWS).astype(BF16)

    def turn_in(a, block):
        return recv[a, part(block)[1]].astype(F32).reshape(128, ROWS)

    def to_stage(a):
        def use(block):
            stage[part(block)[0], :] = turn_in(a, block)

        return use

    def from_stage(a):
        def fill(block):
            send[a, part(block)[1]] = stage[part(block)[0], :].reshape(PLANE, OWN, ROWS).astype(BF16)

        return fill

    def forward(a):
        for p in range(OWN // 2):
            x = jnp.concatenate([stage[pl.ds(2 * p + j, CTX, stride=OWN), :].astype(BF16) for j in (0, 1)], 1)
            waves = dot(outer_ref[...], jnp.concatenate([x, x], 0))
            for j in (0, 1):
                re, im = waves[:CTX, j * ROWS : (j + 1) * ROWS], waves[CTX:, j * ROWS : (j + 1) * ROWS]
                q = jnp.concatenate(
                    [re * twist_ref[0] + im * twist_ref[1], im * twist_ref[0] - re * twist_ref[1]], 1
                )
                at = pl.ds((2 * p + j) * CTX, CTX)
                part_hi[at, :], part_lo[at, :] = split(q)
        for b in range(COLS // 256):
            at = pl.ds(b * 256, 256)
            high = part_hi[at, :]
            spec[a, at, :] = dot(high, dense_ref[0]) + (dot(high, dense_ref[1]) + dot(part_lo[at, :], dense_ref[0]))

    def inverse(first, second, conjugate):
        for b in range(COLS // 256):
            at = pl.ds(b * 256, 256)
            fr, fi = spec[first, at, :ROWS], spec[first, at, ROWS:]
            sr, si = spec[second, at, :ROWS], spec[second, at, ROWS:]
            if conjugate:
                re, im = fr * sr + fi * si, fr * si - fi * sr
            else:
                re, im = fr * sr - fi * si, fr * si + fi * sr
            high, low = split(jnp.concatenate([re, im], 1))
            wide[at, :] = dot(high, turned_ref[0]) + (dot(high, turned_ref[1]) + dot(low, turned_ref[0]))
        for p in range(OWN // 2):
            u = []
            for j in (0, 1):
                at = pl.ds((2 * p + j) * CTX, CTX)
                re, im = wide[at, :ROWS], wide[at, ROWS:]
                u.append(
                    jnp.concatenate(
                        [re * twist_ref[0] - im * twist_ref[1], re * twist_ref[1] + im * twist_ref[0]], 0
                    )
                )
            high, low = split(jnp.concatenate(u, 1))
            y = dot(back_ref[...], jnp.concatenate([high, low, high], 0))
            for j in (0, 1):
                stage[pl.ds(2 * p + j, CTX, stride=OWN), :] = y[:, j * ROWS : (j + 1) * ROWS]

    blocks = range(COLS // 128)

    def turn_filter():
        loads[0].wait()
        for i in blocks:
            turn_out(0, i, taps[:, part(i)[0]].astype(F32))

    def squares():
        loads[1].wait()
        partial = jnp.zeros((8, ROWS), F32)
        for i in blocks:
            turned = jnp.transpose(hidden[:, part(i)[0]].astype(F32))
            hidden_t[part(i)[0], :] = turned
            partial = partial + jnp.sum((turned * turned).reshape(16, 8, ROWS), axis=0)
        sums[0] = partial

    @pl.when(direct)
    def _():
        turn_filter()
        squares()
        pl.semaphore_wait(barrier, CTX - 1 + CH - 1)
        add_up(0)

    @pl.when(plane > AGENT)
    def _():
        pl.semaphore_wait(barrier, CTX - 1)
        agent = AGENT * PLANE + place
        pl.semaphore_signal(relay.at[0], inc=1, device_id={"ctx": agent}, device_id_type=MESH)
        turn_filter()

    exchange(0, lambda block: None)

    @pl.when(plane == AGENT)
    def _():
        pl.semaphore_wait(relay.at[0], PLANES - 1 - AGENT)
        to_channels(relay.at[1])

    @pl.when(plane > AGENT)
    def _():
        squares()
        pl.semaphore_wait(relay.at[2], 1)
        add_up(0)

    loads[2].wait()
    loads[3].wait()

    def conv_grad(block):
        at = part(block)[0]
        turn_out(1, block, upstream[:, at].astype(F32) * gating[:, at].astype(F32))

    exchange(1, conv_grad)

    @pl.when(plane == AGENT)
    def _():
        pl.semaphore_wait(relay.at[1], CH - 1)
        for later in range(AGENT + 1, PLANES):
            peer = later * PLANE + place
            pl.semaphore_signal(relay.at[2], inc=1, device_id={"ctx": peer}, device_id_type=MESH)

    loads[4].wait()
    for i in blocks:
        at = part(i)[0]
        gain_t[at, :] = jnp.transpose(jnp.broadcast_to(gain_ref[:, at], (ROWS, 128)))
    for load in loads[5:]:
        load.wait()
    high, low = split(outer_f32[...])
    outer_ref[...] = jnp.concatenate([high, low], 1)
    high, low = split(back_f32[...])
    back_ref[...] = jnp.concatenate([high, high, low], 1)
    dense_ref[0], dense_ref[1] = split(dense_f32[...])
    turned_ref[0], turned_ref[1] = split(turned_f32[...])

    arrivals(0, to_stage(0))
    forward(0)
    inverse_rms = lax.rsqrt(added(0) + EPSILON)

    def mixed(block):
        at, owners = part(block)
        normed = hidden_t[at, :] * inverse_rms
        hidden_t[at, :] = normed
        send[2, owners] = (normed * gain_t[at, :]).astype(BF16).reshape(PLANE, OWN, ROWS)

    exchange(2, mixed)

    arrivals(1, to_stage(1))
    forward(1)
    inverse(0, 1, True)
    exchange(3, from_stage(3))
    arrivals(2, to_stage(2))
    forward(2)
    inverse(2, 0, False)
    exchange(4, from_stage(4))
    inverse(2, 1, True)

    sums[1] = jnp.zeros((8, ROWS), F32)

    def project(block):
        at = part(block)[0]
        scaled = turn_in(3, block) * gain_t[at, :]
        gain_t[at, :] = scaled
        sums[1] = sums[1] + jnp.sum((scaled * hidden_t[at, :]).reshape(16, 8, ROWS), axis=0)

    arrivals(3, project)
    add_up(1)
    exchange(5, from_stage(5))

    def gated(block):
        at = part(block)[0]
        value = jnp.transpose(turn_in(4, block))
        output[:, at] = (gating[:, at].astype(F32) * value).astype(BF16)
        gate_grad[:, at] = (upstream[:, at].astype(F32) * value).astype(BF16)

    arrivals(4, gated)
    projection = added(1)
    for i in blocks:
        at = part(i)[0]
        value = inverse_rms * (gain_t[at, :] - hidden_t[at, :] * projection)
        hidden_grad[:, at] = jnp.transpose(value).astype(BF16)

    def taps_grad(block):
        filter_grad[:, part(block)[0]] = jnp.transpose(turn_in(5, block)).astype(BF16)

    arrivals(5, taps_grad)

    for a in range(6):
        sent(a)
    for which in (0, 1):
        whole_sum(which).wait_send()


def finish(*refs):
    copies = [pltpu.make_async_copy(refs[i], refs[4 + i], refs[8].at[i]) for i in range(4)]
    for copy in copies:
        copy.start()
    for copy in copies:
        copy.wait()


def shards(hidden, gating, filter_taps, norm_gain, upstream):
    consts = [jnp.asarray(t) for t in tables()]
    vmem, hbm = pl.BlockSpec(memory_space=pltpu.VMEM), pl.BlockSpec(memory_space=pltpu.HBM)
    block = pltpu.VMEM((ROWS, COLS), BF16)
    gain = norm_gain.reshape(1, COLS)
    results = pl.pallas_call(
        kernel,
        out_shape=(pltpu.VMEM((ROWS, COLS), BF16),) * 4,
        in_specs=[hbm] * 10,
        out_specs=(vmem,) * 4,
        scratch_shapes=[block] * 4
        + [pltpu.VMEM(t.shape, t.dtype) for t in (gain, *consts)]
        + [
            pltpu.VMEM((2 * CTX, 2 * CTX), BF16),
            pltpu.VMEM((CTX, 6 * CTX), BF16),
            pltpu.VMEM((2, 2 * ROWS, 2 * ROWS), BF16),
            pltpu.VMEM((2, 2 * ROWS, 2 * ROWS), BF16),
            pltpu.VMEM((6, CTX, OWN, ROWS), BF16),
            pltpu.VMEM((6, CTX, OWN, ROWS), BF16),
            pltpu.VMEM((3, COLS, 2 * ROWS), F32),
            pltpu.VMEM((COLS, 2 * ROWS), BF16),
            pltpu.VMEM((COLS, 2 * ROWS), BF16),
            pltpu.VMEM((COLS, 2 * ROWS), F32),
            pltpu.VMEM((COLS, ROWS), F32),
            pltpu.VMEM((COLS, ROWS), F32),
            pltpu.VMEM((COLS, ROWS), F32),
            pltpu.VMEM((2, 8, ROWS), F32),
            pltpu.VMEM((2, CH, 8, ROWS), F32),
            pltpu.SemaphoreType.DMA((10,)),
            pltpu.SemaphoreType.DMA((6,)),
            pltpu.SemaphoreType.DMA((6, PLANES)),
            pltpu.SemaphoreType.DMA((2,)),
            pltpu.SemaphoreType.DMA((2,)),
            pltpu.SemaphoreType.REGULAR((3,)),
        ],
        compiler_params=pltpu.CompilerParams(collective_id=0, has_side_effects=True, vmem_limit_bytes=VMEM_BYTES),
    )(hidden, gating, filter_taps, upstream, gain, *consts)
    return pl.pallas_call(
        finish,
        out_shape=(pltpu.HBM((ROWS, COLS), BF16),) * 4,
        in_specs=[vmem] * 4,
        out_specs=(hbm,) * 4,
        scratch_shapes=[pltpu.SemaphoreType.DMA((4,))],
        compiler_params=pltpu.CompilerParams(vmem_limit_bytes=1 << 20),
    )(*results)


def solution(mesh):
    spec = P("ctx", "ch")
    return jax.shard_map(
        shards, mesh=mesh, in_specs=(spec, spec, spec, P("ch"), spec), out_specs=(spec,) * 4, check_vma=False
    )
```
